512 devices in a mesh: seq: 64 (over x, z, core), head: 8 (over y).
Axes of the slice: x: 4, y: 8, z: 8, core: 2. Of those that a mesh axis runs over, the one named last changes fastest.
Arguments:
- queries: bfloat16 [40960, 5120], P(('seq', 'head')), may hold values from -128 to 128
- keys: bfloat16 [40960, 5120], P(('seq', 'head')), may hold values from -128 to 128
- values: bfloat16 [40960, 5120], P(('seq', 'head')), may hold values from -6 to 6
- query_gain: float32 [5120], replicated, may hold values from 1 to 4
- key_gain: float32 [5120], replicated, may hold values from 1 to 4
- level_gate: float32 [30, 5120], replicated, may hold values from -4 to 4
- clip_lengths: int32 [16, 4], replicated, may hold values from 1 to 960, 2560 in all within a row
- levels: int32 [16, 4], replicated, may hold values from 0 to 29, as said below
Outputs:
- gated_output: bfloat16 [40960, 5120], P(('seq', 'head'))
The draws below stay inside these ranges and needn't reach their ends.
Inputs may be any that keep to these rules, and one draw needn't show every extreme that they name: `clip_lengths`: each row sums to 2560; its largest entry is 960. Along each row the levels never fall; the first is 0, the third is above 0, the last is 29.
All inputs are finite; a program needn't handle non-finite values.
Results may differ from the reference program's by a relative error of at most 0.012.
The reference program's roundings to bfloat16 on the way count: a program that leaves them out, or rounds other values in their place, can miss the bound.
Values may be sent and summed in bfloat16 or wider, within the bound.
No kernel may reach another device: no remote copies, remote signals or barrier semaphores. Data moves between devices by JAX's collectives and lax.ppermute only.
A program may use at most 128 MiB of HBM per device.

```python
import math
import jax
import jax.numpy as jnp
import numpy as np
from jax import lax

H = 40
HD = 128
D = 5120
GROUP = 4
CLIPS = 4
LEVELS = 30
ROWS = 640
SEQS = 16
SEQ_LEN = 2560
TOKENS = 40960
MOST = 960


def log_spread(key, shape, lower, upper):
    return jnp.exp(jax.random.uniform(key, shape, jnp.float32, math.log(lower), math.log(upper)))


def draw_queries(key, part):
    key = jax.random.fold_in(key, 11)
    key_col, key_row, key_base = jax.random.split(key, 3)
    column_scale = log_spread(key_col, (1, D), 0.3, 3.0)
    row_scale = log_spread(key_row, (TOKENS, 1), 0.3, 3.0)
    field_rows = jax.random.normal(key_base, (TOKENS, D), jnp.float32) * column_scale * row_scale
    return jnp.clip(field_rows, -128.0, 128.0).astype(jnp.bfloat16)


def draw_keys(key, part):
    key = jax.random.fold_in(key, 12)
    key_col, key_row, key_base = jax.random.split(key, 3)
    column_scale = log_spread(key_col, (1, D), 0.3, 3.0)
    row_scale = log_spread(key_row, (TOKENS, 1), 0.3, 3.0)
    field_rows = jax.random.normal(key_base, (TOKENS, D), jnp.float32) * column_scale * row_scale
    return jnp.clip(field_rows, -128.0, 128.0).astype(jnp.bfloat16)


def draw_levels(key, part):
    key = jax.random.fold_in(key, 13)
    key_noisy, key_clean = jax.random.split(key, 2)
    noisy_levels = jnp.sort(jax.random.randint(key_noisy, (SEQS, 2), 1, LEVELS), axis=1)
    clean_second = jax.random.randint(key_clean, (SEQS,), 0, 2)
    second_level = jnp.where(clean_second == 1, 0, noisy_levels[:, 0])
    first_level = jnp.zeros((SEQS,), jnp.int32)
    last_level = jnp.full((SEQS,), LEVELS - 1, jnp.int32)
    return jnp.stack((first_level, second_level, noisy_levels[:, 1], last_level), axis=1).astype(jnp.int32)


def block_scale(rng, dims, shards, low, top_value):
    def one(position, blocks):
        steps = jax.random.uniform(jax.random.fold_in(jax.random.fold_in(rng, 6), position), (blocks,), jnp.float32, low / len(shards), top_value / len(shards))
        return jnp.repeat(jnp.exp(steps), dims[position] // blocks).reshape((-1,) + (1,) * (len(dims) - position - 1))

    gain = one(*shards[0])
    for cut in shards[1:]:
        gain = gain * one(*cut)
    return gain


def split_up(number_of, total, reach, skew):
    loads = [(1 << 20) // math.isqrt(rank ** skew) + 1 for rank in range(2, number_of + 1)]
    surplus, counts = total - reach - (number_of - 1), [1] * (number_of - 1)
    while surplus > 0:
        movable = [i for i in range(number_of - 1) if counts[i] < reach]
        mass, budget = sum([loads[i] for i in movable]), surplus
        for i in movable:
            more = min(reach - counts[i], max(1, budget * loads[i] // mass), surplus)
            counts[i] = counts[i] + more
            surplus = surplus - more
    return np.array([reach] + counts)


def uneven_parts(key, count, total, most, skew):
    if count == 2:
        one = jax.random.randint(key, (), max(1, total - most), min(most, total - 1) + 1)
        return jnp.stack([one, total - one])
    tallies = jnp.asarray(split_up(count, total, most, skew), jnp.int32)
    twos = (count - 1) // 2
    donor, receiver = tallies[1:1 + 2 * twos:2], tallies[2:2 + 2 * twos:2]
    slack = jnp.minimum(donor - 1, most - receiver)
    moved = jax.random.randint(jax.random.fold_in(key, 1), (twos,), 0, 1 << 20) % (slack + 1)
    tallies = tallies.at[1:1 + 2 * twos:2].set(donor - moved).at[2:2 + 2 * twos:2].set(receiver + moved)
    return tallies[jax.random.permutation(jax.random.fold_in(key, 2), count)]


def noise(own_key, extent, width, limit, shards=(), kind=jnp.bfloat16):
    gain = block_scale(own_key, extent, shards, -0.22, 0.18) if shards else 1.0
    drawn = jax.random.normal(own_key, extent, jnp.float32) * width * gain
    return jnp.minimum(jnp.maximum(drawn, -limit), limit).astype(kind)


def setup_inputs(seed: int = 0) -> dict:
    key_of = jax.random.split(jax.random.key(seed), 9)
    queries = draw_queries(jax.random.fold_in(key_of[8], 71), 0)
    keys = draw_keys(jax.random.fold_in(key_of[8], 71), 0)
    values = noise(key_of[2], (TOKENS, D), 1.0, 6.0, ((0, 512),))
    query_gain = jnp.clip(jnp.exp(jax.random.uniform(key_of[3], (D,), jnp.float32, math.log(1.0), math.log(4.0))), 1.0, 4.0)
    key_gain = jnp.clip(jnp.exp(jax.random.uniform(key_of[4], (D,), jnp.float32, math.log(1.0), math.log(4.0))), 1.0, 4.0)
    level_gate = noise(key_of[5], (LEVELS, D), 1.0, 4.0, (), jnp.float32)
    clip_lengths = jax.vmap(lambda own: uneven_parts(own, CLIPS, SEQ_LEN, MOST, 0))(jax.random.split(key_of[6], SEQS)).reshape((SEQS, CLIPS)).astype(jnp.int32)
    levels = draw_levels(jax.random.fold_in(key_of[8], 71), 0)
    return {"queries": queries, "keys": keys, "values": values, "query_gain": query_gain, "key_gain": key_gain, "level_gate": level_gate, "clip_lengths": clip_lengths, "levels": levels}


epsilon = 1e-06

def normalize(token_rows, gain_vector):
    widened = token_rows.astype(jnp.float32)
    inverse_rms = lax.rsqrt(lax.optimization_barrier(jnp.mean(widened * widened, axis=1, keepdims=True)) + epsilon)
    return (widened * inverse_rms * gain_vector[None, :]).astype(jnp.bfloat16)

def clip_index(positions, clip_ends):
    result = jnp.zeros(positions.shape, jnp.int32)
    for boundary in range(clip_ends.shape[0] - 1):
        result = result + (positions >= clip_ends[boundary]).astype(jnp.int32)
    return result

def clip_value(clip_ids, clip_table):
    result = jnp.zeros(clip_ids.shape, clip_table.dtype)
    for clip_id in range(clip_table.shape[0]):
        result = jnp.where(clip_ids == clip_id, clip_table[clip_id], result)
    return result

def video_major(stacked):
    feature_count = stacked.shape[-1]
    return stacked.reshape(GROUP, SEQS, ROWS, feature_count).transpose(1, 0, 2, 3).reshape(SEQS, SEQ_LEN, feature_count)

def reference(queries, keys, values, query_gain, key_gain, level_gate, clip_lengths, levels):
    normed_q = video_major(normalize(queries, query_gain))
    normed_k = video_major(normalize(keys, key_gain))
    value_rows = video_major(values)
    positions = jnp.arange(SEQ_LEN, dtype=jnp.int32)
    inv_root = 1.0 / math.sqrt(HD)

    def single_video(packed):
        video_q, video_k, video_v, lengths_row, levels_row = packed
        clip_ids = clip_index(positions, jnp.cumsum(lengths_row))
        allowed = clip_ids[None, :] <= clip_ids[:, None]

        def single_head(triple):
            head_q, head_k, head_v = triple
            scores = jnp.dot(head_q, head_k.T, preferred_element_type=jnp.float32) * inv_root
            scores = jnp.where(allowed, scores, -jnp.inf)
            weights = jnp.exp(scores - lax.optimization_barrier(jnp.max(scores, axis=1, keepdims=True)))
            row_sum = lax.optimization_barrier(jnp.sum(weights, axis=1, keepdims=True))
            weighted = jnp.dot(weights.astype(jnp.bfloat16), head_v, preferred_element_type=jnp.float32)
            return (weighted / row_sum).astype(jnp.bfloat16)
        split_heads = (video_q.reshape(SEQ_LEN, H, HD).transpose(1, 0, 2), video_k.reshape(SEQ_LEN, H, HD).transpose(1, 0, 2), video_v.reshape(SEQ_LEN, H, HD).transpose(1, 0, 2))
        attended = lax.map(single_head, split_heads).transpose(1, 0, 2).reshape(SEQ_LEN, H * HD)
        token_levels = clip_value(clip_ids, levels_row)
        gate_rows = level_gate[token_levels]
        gated_rows = jnp.where((token_levels > 0)[:, None], gate_rows * attended.astype(jnp.float32), 0.0)
        return gated_rows.astype(jnp.bfloat16)
    gated_rows = lax.map(single_video, (normed_q, normed_k, value_rows, clip_lengths, levels))
    return gated_rows.reshape(SEQS, GROUP, ROWS, H * HD).transpose(1, 0, 2, 3).reshape(TOKENS, H * HD)
```

```python
import functools
import math

import jax
import jax.numpy as jnp
from jax import lax
from jax.experimental import pallas as pl
from jax.experimental.pallas import tpu as pltpu
from jax.sharding import Mesh
from jax.sharding import PartitionSpec as P

HD = 128
GROUP = 4
CLIPS = 4
PLANE = 32
EXTRA = 8

epsilon = 1e-06
very_negative = -1e30
exponent_scale = math.log2(math.e) / math.sqrt(HD)

VMEM_BYTES = 56 * 1024 * 1024


def vmem():
    return pl.BlockSpec(memory_space=pltpu.VMEM)


def smem():
    return pl.BlockSpec(memory_space=pltpu.SMEM)


def normalize_kernel(q_ref, k_ref, v_ref, qg_ref, kg_ref, own_ref, extra_ref):
    rows, width = q_ref.shape

    def inverse_rms(ref):
        total = jnp.zeros((rows, HD), jnp.float32)
        for head in range(width // HD):
            block = ref[:, head * HD : (head + 1) * HD].astype(jnp.float32)
            total = total + block * block
        mean = jnp.sum(total, axis=1, keepdims=True) / width
        return jnp.broadcast_to(lax.rsqrt(mean + epsilon), (rows, HD))

    inverse_q, inverse_k = inverse_rms(q_ref), inverse_rms(k_ref)
    for head in range(PLANE + EXTRA):
        target, place = (own_ref, head) if head < PLANE else (extra_ref, head - PLANE)
        columns = slice(head * HD, (head + 1) * HD)
        for part, (ref, gain_ref, inverse) in enumerate(
            ((q_ref, qg_ref, inverse_q), (k_ref, kg_ref, inverse_k))
        ):
            block = ref[:, columns].astype(jnp.float32)
            target[place, part] = (block * inverse * gain_ref[:, columns]).astype(jnp.bfloat16)
        target[place, 2] = v_ref[:, columns]


def normalize(queries, keys, values, query_gain, key_gain):
    rows = queries.shape[0]
    return pl.pallas_call(
        normalize_kernel,
        out_shape=[
            jax.ShapeDtypeStruct((PLANE, 3, rows, HD), jnp.bfloat16),
            jax.ShapeDtypeStruct((EXTRA, 3, rows, HD), jnp.bfloat16),
        ],
        in_specs=[vmem()] * 5,
        out_specs=[vmem()] * 2,
        compiler_params=pltpu.CompilerParams(vmem_limit_bytes=VMEM_BYTES),
        cost_estimate=pl.CostEstimate(flops=5_000_000, bytes_accessed=5_000_000, transcendentals=160),
    )(queries, keys, values, query_gain[None, :], key_gain[None, :])


def clip_of(positions, ends):
    result = jnp.zeros_like(positions)
    for boundary in range(CLIPS - 1):
        result = result + (positions >= ends[boundary]).astype(jnp.int32)
    return result


def pick(clip_ids, options):
    result = options[0]
    for clip_id in range(1, CLIPS):
        result = jnp.where(clip_ids == clip_id, options[clip_id], result)
    return result


def clip_table(lengths_ref, levels_ref):
    video = lax.axis_index("v")
    ends, total = [], 0
    for clip_id in range(CLIPS):
        total = total + lengths_ref[video, clip_id]
        ends.append(total)
    return ends, [levels_ref[video, clip_id] for clip_id in range(CLIPS)]


def blocked_columns(positions, ends):
    lanes = lax.broadcasted_iota(jnp.int32, positions.shape, 1)
    later = jnp.logical_and(clip_of(positions, ends) > lanes, lanes < CLIPS)
    return jnp.where(later, very_negative, 0.0).astype(jnp.bfloat16)


def clip_columns(clip_ids):
    lanes = lax.broadcasted_iota(jnp.int32, clip_ids.shape, 1)
    return jnp.where(clip_ids == lanes, 1.0, 0.0).astype(jnp.bfloat16)


def attend(query_block, positions, last, key_ref, value_of, score_ref, chunk, ends, levels, gates, write):
    rows, length = score_ref.shape
    clip_ids = clip_of(positions, ends)
    last_clip = clip_of(last, ends)
    live = pick(last_clip, levels) > 0
    chunks = (pick(last_clip, ends) + chunk - 1) // chunk

    def fold(count, extended):
        peak = jnp.full((rows, HD), very_negative, jnp.float32)
        for step in range(count):
            scores = lax.dot_general(
                extended,
                key_ref[step * chunk : (step + 1) * chunk, :],
                (((1,), (1,)), ((), ())),
                preferred_element_type=jnp.float32,
            )
            score_ref[:, step * chunk : (step + 1) * chunk] = scores
            for part in range(chunk // HD):
                peak = jnp.maximum(peak, scores[:, part * HD : (part + 1) * HD])
        peak = jnp.max(peak, axis=1, keepdims=True) * exponent_scale
        peak = jnp.broadcast_to(peak, (rows, HD))
        total = jnp.zeros((rows, HD), jnp.float32)
        weighted = jnp.zeros((rows, HD), jnp.float32)
        for step in range(count):
            rounded = []
            for part in range(chunk // HD):
                start = step * chunk + part * HD
                weights = jnp.exp2(score_ref[:, start : start + HD] * exponent_scale - peak)
                total = total + weights
                rounded.append(weights.astype(jnp.bfloat16))
            weighted = weighted + jnp.dot(
                jnp.concatenate(rounded, axis=1),
                value_of(step),
                preferred_element_type=jnp.float32,
            )
        attention = weighted / jnp.sum(total, axis=1, keepdims=True)
        attention = attention.astype(jnp.bfloat16).astype(jnp.float32)
        gated = pick(clip_ids, [gates(level) for level in levels]) * attention
        gated = jnp.where(pick(clip_ids, levels) > 0, gated, 0.0)
        write(gated.astype(jnp.bfloat16))

    @pl.when(live)
    def _():
        extended = jnp.concatenate([query_block(), clip_columns(clip_ids)], axis=1)
        for count in range(1, length // chunk + 1):
            pl.when(chunks == count)(functools.partial(fold, count, extended))

    @pl.when(jnp.logical_not(live))
    def _():
        write(jnp.zeros((rows, HD), jnp.bfloat16))


def attention_kernel(
    lengths_ref, levels_ref, gate_ref, query_ref, held_ref, out_ref, key_ref, score_ref, level_ref,
    *, head_of, first_of, places, chunk,
):
    query_place, key_place, value_place = places
    blocks, _, block_rows, _ = query_ref.shape
    rows, length = score_ref.shape
    tile_blocks, chunk_blocks = rows // block_rows, chunk // block_rows
    ends, levels = clip_table(lengths_ref, levels_ref)
    level_ref[...] = gate_ref[:, pl.ds(pl.multiple_of(head_of() * HD, HD), HD)]

    def fill(step, _):
        start = pl.multiple_of(step * chunk, chunk)
        key_ref[pl.ds(start, chunk), 0:HD] = held_ref[
            pl.ds(step * chunk_blocks, chunk_blocks), key_place
        ].reshape(chunk, HD)
        positions = start + lax.broadcasted_iota(jnp.int32, (chunk, HD), 0)
        key_ref[pl.ds(start, chunk), HD : 2 * HD] = blocked_columns(positions, ends)
        return 0

    lax.fori_loop(0, length // chunk, fill, 0)

    def tile(index, _):
        first = first_of() + index * rows
        blocks_here = pl.ds(index * tile_blocks, tile_blocks)

        def write(gated):
            out_ref[blocks_here] = gated.reshape(tile_blocks, block_rows, HD)

        attend(
            lambda: query_ref[blocks_here, query_place].reshape(rows, HD),
            first + lax.broadcasted_iota(jnp.int32, (rows, HD), 0),
            first + rows - 1,
            key_ref,
            lambda step: held_ref[
                step * chunk_blocks : (step + 1) * chunk_blocks, value_place
            ].reshape(chunk, HD),
            score_ref,
            chunk,
            ends,
            levels,
            lambda level: level_ref[pl.ds(level, 1), :],
            write,
        )
        return 0

    lax.fori_loop(0, blocks * block_rows // rows, tile, 0)


def attention(clip_lengths, levels, level_gate, queries, held, head_of, first_of, places, rows=320, chunk=640):
    blocks, _, block_rows, _ = queries.shape
    length = held.shape[0] * block_rows
    work = blocks * block_rows * length
    return pl.pallas_call(
        functools.partial(
            attention_kernel, head_of=head_of, first_of=first_of, places=places, chunk=chunk
        ),
        out_shape=jax.ShapeDtypeStruct((blocks, block_rows, HD), jnp.bfloat16),
        in_specs=[smem(), smem(), vmem(), vmem(), vmem()],
        out_specs=vmem(),
        scratch_shapes=[
            pltpu.VMEM((length, 2 * HD), jnp.bfloat16),
            pltpu.VMEM((rows, length), jnp.float32),
            pltpu.VMEM((level_gate.shape[0], HD), jnp.float32),
        ],
        compiler_params=pltpu.CompilerParams(vmem_limit_bytes=VMEM_BYTES),
        cost_estimate=pl.CostEstimate(
            flops=1200 * work, bytes_accessed=3_000_000, transcendentals=work
        ),
    )(clip_lengths, levels, level_gate, queries, held)


def assemble_kernel(own_ref, extra_ref, out_ref):
    for head in range(PLANE):
        out_ref[:, head * HD : (head + 1) * HD] = own_ref[head]
    for head in range(EXTRA):
        out_ref[:, (PLANE + head) * HD : (PLANE + head + 1) * HD] = extra_ref[head]


def assemble(own, extra):
    rows = own.shape[1]
    return pl.pallas_call(
        assemble_kernel,
        out_shape=jax.ShapeDtypeStruct((rows, (PLANE + EXTRA) * HD), jnp.bfloat16),
        in_specs=[vmem()] * 2,
        out_specs=vmem(),
        compiler_params=pltpu.CompilerParams(vmem_limit_bytes=VMEM_BYTES),
        cost_estimate=pl.CostEstimate(flops=0, bytes_accessed=1_700_000, transcendentals=0),
    )(own, extra)


def local(queries, keys, values, query_gain, key_gain, level_gate, clip_lengths, levels):
    own, extra = normalize(queries, keys, values, query_gain, key_gain)
    extra_held = lax.all_to_all(extra, "y", 0, 0, tiled=True)
    own_held = lax.all_to_all(own, ("x", "y"), 0, 0, tiled=True)
    gathered = lax.all_gather(extra_held[:, 1:], "x", axis=0, tiled=True)
    table = (clip_lengths, levels, level_gate)
    extra_out = attention(
        *table,
        extra_held,
        gathered,
        head_of=lambda: PLANE + lax.axis_index("y"),
        first_of=lambda: lax.axis_index("x") * 640,
        places=(0, 0, 1),
    )
    extra_back = lax.all_to_all(extra_out, "y", 0, 0, tiled=True)
    own_out = attention(
        *table,
        own_held,
        own_held,
        head_of=lambda: lax.axis_index("x") * 8 + lax.axis_index("y"),
        first_of=lambda: 0,
        places=(0, 1, 2),
    )
    own_back = lax.all_to_all(own_out, ("x", "y"), 0, 0, tiled=True)
    return assemble(own_back, extra_back)


def solution(mesh):
    videos = mesh.shape["seq"] // GROUP
    finer = Mesh(mesh.devices.reshape(GROUP, videos, EXTRA), ("x", "v", "y"))
    rows = P(("x", "v", "y"), None)
    return jax.shard_map(
        local,
        mesh=finer,
        in_specs=(rows, rows, rows, P(), P(), P(), P(), P()),
        out_specs=rows,
        check_vma=False,
    )
```

```python
import functools
import math

import jax
import jax.numpy as jnp
from jax import lax
from jax.experimental import pallas as pl
from jax.experimental.pallas import tpu as pltpu
from jax.sharding import Mesh
from jax.sharding import PartitionSpec as P

HD = 128
GROUP = 4
CLIPS = 4
PLANE = 32
EXTRA = 8

epsilon = 1e-06
very_negative = -1e30
exponent_scale = math.log2(math.e) / math.sqrt(HD)

VMEM_BYTES = 24 * 1024 * 1024
LARGE_VMEM = 56 * 1024 * 1024
SMALL_VMEM = 12 * 1024 * 1024


def vmem():
    return pl.BlockSpec(memory_space=pltpu.VMEM)


def smem():
    return pl.BlockSpec(memory_space=pltpu.SMEM)


def inverse_rms(ref):
    rows, width = ref.shape
    total = jnp.zeros((rows, HD), jnp.float32)
    for head in range(width // HD):
        block = ref[:, head * HD : (head + 1) * HD].astype(jnp.float32)
        total = total + block * block
    mean = jnp.sum(total, axis=1, keepdims=True) / width
    return jnp.broadcast_to(lax.rsqrt(mean + epsilon), (rows, HD))


def lay_out(q_ref, k_ref, v_ref, qg_ref, kg_ref, inverses, out_ref):
    for head in range(out_ref.shape[0]):
        columns = slice(head * HD, (head + 1) * HD)
        for part, (ref, gain_ref, inverse) in enumerate(
            ((q_ref, qg_ref, inverses[0]), (k_ref, kg_ref, inverses[1]))
        ):
            block = ref[:, columns].astype(jnp.float32)
            out_ref[head, part] = (block * inverse * gain_ref[:, columns]).astype(jnp.bfloat16)
        out_ref[head, 2] = v_ref[:, columns]


def extra_norm_kernel(q_ref, k_ref, v_ref, qg_ref, kg_ref, out_ref, inverse_ref):
    inverses = [inverse_rms(q_ref), inverse_rms(k_ref)]
    inverse_ref[0], inverse_ref[1] = inverses
    columns = slice(PLANE * HD, (PLANE + EXTRA) * HD)
    lay_out(q_ref.at[:, columns], k_ref.at[:, columns], v_ref, qg_ref, kg_ref, inverses, out_ref)


def own_norm_kernel(q_ref, k_ref, v_ref, qg_ref, kg_ref, inverse_ref, out_ref):
    inverses = [inverse_ref[0], inverse_ref[1]]
    lay_out(q_ref, k_ref, v_ref, qg_ref, kg_ref, inverses, out_ref)


def normalize(queries, keys, values, query_gain, key_gain):
    rows, width = queries.shape
    own_width, extra_width = PLANE * HD, EXTRA * HD

    def block(height, count, place=0):
        return pl.BlockSpec((height, count), lambda step: (0, place))

    def full(*shape):
        return pl.BlockSpec(shape, lambda step: (0,) * len(shape))

    whole = (queries, keys, values, query_gain[None, :], key_gain[None, :])
    params = pltpu.CompilerParams(vmem_limit_bytes=LARGE_VMEM)
    last = own_width // extra_width
    extra, inverses = pl.pallas_call(
        extra_norm_kernel,
        grid=(1,),
        out_shape=[
            jax.ShapeDtypeStruct((EXTRA, 3, rows, HD), jnp.bfloat16),
            jax.ShapeDtypeStruct((2, rows, HD), jnp.float32),
        ],
        in_specs=[block(rows, width)] * 2
        + [block(rows, extra_width, last)]
        + [block(1, extra_width, last)] * 2,
        out_specs=[full(EXTRA, 3, rows, HD), full(2, rows, HD)],
        compiler_params=params,
        cost_estimate=pl.CostEstimate(flops=3_000_000, bytes_accessed=3_000_000, transcendentals=160),
    )(*whole)
    own = pl.pallas_call(
        own_norm_kernel,
        grid=(1,),
        out_shape=jax.ShapeDtypeStruct((PLANE, 3, rows, HD), jnp.bfloat16),
        in_specs=[block(rows, own_width)] * 3 + [block(1, own_width)] * 2 + [full(2, rows, HD)],
        out_specs=full(PLANE, 3, rows, HD),
        compiler_params=params,
        cost_estimate=pl.CostEstimate(flops=3_000_000, bytes_accessed=5_000_000, transcendentals=0),
    )(*whole, inverses)
    return own, extra


def clip_of(positions, ends):
    result = jnp.zeros_like(positions)
    for boundary in range(CLIPS - 1):
        result = result + (positions >= ends[boundary]).astype(jnp.int32)
    return result


def pick(clip_ids, options):
    result = options[0]
    for clip_id in range(1, CLIPS):
        result = jnp.where(clip_ids == clip_id, options[clip_id], result)
    return result


def clip_table(lengths_ref, levels_ref):
    video = lax.axis_index("v")
    ends, total = [], 0
    for clip_id in range(CLIPS):
        total = total + lengths_ref[clip_id, video]
        ends.append(total)
    return ends, [levels_ref[clip_id, video] for clip_id in range(CLIPS)]


def blocked_rows(start, count, ends):
    clip_ids = clip_of(start + lax.broadcasted_iota(jnp.int32, (16, count), 1), ends)
    rows = lax.broadcasted_iota(jnp.int32, (16, count), 0)
    later = jnp.logical_and(clip_ids > rows, rows < CLIPS)
    return jnp.where(later, very_negative, 0.0).astype(jnp.bfloat16)


def clip_columns(clip_ids):
    lanes = lax.broadcasted_iota(jnp.int32, clip_ids.shape, 1)
    return jnp.where(clip_ids == lanes, 1.0, 0.0).astype(jnp.bfloat16)


def attention_kernel(
    lengths_ref, levels_ref, gate_ref, query_ref, *refs, piece_count, first_of, places, chunk
):
    piece_refs, (out_ref, key_ref, value_ref, score_ref) = refs[:piece_count], refs[piece_count:]
    query_place, key_place, value_place = places
    blocks, _, block_rows, _ = query_ref.shape
    rows, _ = score_ref.shape
    tile_blocks, chunk_blocks = rows // block_rows, chunk // block_rows
    tiles = blocks // tile_blocks
    ends, levels = clip_table(lengths_ref, levels_ref)

    length, piece_rows = key_ref.shape[1], key_ref.shape[1] // piece_count
    for turn, piece_ref in enumerate(piece_refs):
        place = (lax.axis_index("x") + GROUP - turn) % GROUP if piece_count > 1 else 0
        for step in range(piece_rows // chunk):
            start = place * piece_rows + step * chunk
            where = pl.ds(pl.multiple_of(start, chunk), chunk)
            source = slice(step * chunk_blocks, (step + 1) * chunk_blocks)
            key_ref[0:HD, where] = piece_ref[source, key_place].reshape(chunk, HD).T
            key_ref[HD : HD + 16, where] = blocked_rows(start, chunk, ends)
            if piece_count > 1:
                value_ref[where, :] = piece_ref[source, value_place].reshape(chunk, HD)
    key_ref[HD + 16 :, :] = jnp.zeros((HD - 16, length), jnp.bfloat16)

    def values_of(step):
        if piece_count > 1:
            return value_ref[step * chunk : (step + 1) * chunk, :]
        return piece_refs[0][step * chunk_blocks : (step + 1) * chunk_blocks, value_place].reshape(chunk, HD)

    def first_row(tile):
        return first_of() + tile * rows

    def last_clip(tile):
        return clip_of(first_row(tile) + rows - 1, ends)

    def chunk_count(tile):
        return (pick(last_clip(tile), ends) + chunk - 1) // chunk

    def clips_of_rows(tile):
        return clip_of(first_row(tile) + lax.broadcasted_iota(jnp.int32, (rows, HD), 0), ends)

    def blocks_of(tile):
        return pl.ds(tile * tile_blocks, tile_blocks)

    def queries_of(tile):
        held = query_ref[blocks_of(tile), query_place].reshape(rows, HD)
        return jnp.concatenate([held, clip_columns(clips_of_rows(tile))], axis=1)

    def whole(tile, count):
        extended = queries_of(tile)
        peak = jnp.full((rows, HD), very_negative, jnp.float32)
        for step in range(count):
            here = slice(step * chunk, (step + 1) * chunk)
            scores = jnp.dot(extended, key_ref[:, here], preferred_element_type=jnp.float32)
            score_ref[:, here] = scores
            for part in range(chunk // HD):
                peak = jnp.maximum(peak, scores[:, part * HD : (part + 1) * HD])
        peak = jnp.max(peak, axis=1, keepdims=True) * exponent_scale
        peak = jnp.broadcast_to(peak, (rows, HD))
        total = jnp.zeros((rows, HD), jnp.float32)
        weighted = jnp.zeros((rows, HD), jnp.float32)
        for step in range(count):
            rounded = []
            for part in range(chunk // HD):
                start = step * chunk + part * HD
                weights = jnp.exp2(score_ref[:, start : start + HD] * exponent_scale - peak)
                total = total + weights
                rounded.append(weights.astype(jnp.bfloat16))
            weighted = weighted + jnp.dot(
                jnp.concatenate(rounded, axis=1), values_of(step), preferred_element_type=jnp.float32
            )
        attention = weighted / jnp.sum(total, axis=1, keepdims=True)
        attention = attention.astype(jnp.bfloat16).astype(jnp.float32)
        positions = first_row(tile) + lax.broadcasted_iota(jnp.int32, (rows, HD), 0)
        gate = gates[0]
        for clip_id in range(1, CLIPS):
            gate = jnp.where(positions >= ends[clip_id - 1], gates[clip_id], gate)
        gated = (gate * attention).astype(jnp.bfloat16)
        out_ref[blocks_of(tile)] = gated.reshape(tile_blocks, block_rows, HD)

    gates = [
        jnp.where(level > 0, gate_ref[pl.ds(level, 1), :], 0.0) for level in levels
    ]
    skipped = 0
    for tile in range(tiles):
        skipped = skipped + (pick(last_clip(tile), levels) <= 0).astype(jnp.int32)

    def clear(tile, _):
        out_ref[blocks_of(tile)] = jnp.zeros((tile_blocks, block_rows, HD), jnp.bfloat16)
        return 0

    def one(tile, _):
        needed = chunk_count(tile)
        for count in range(1, length // chunk + 1):
            pl.when(needed == count)(functools.partial(whole, tile, count))
        return 0

    lax.fori_loop(0, skipped, clear, 0)
    lax.fori_loop(skipped, tiles, one, 0)


def attention(
    clip_lengths, levels, level_gate, queries, pieces, first_of, places, rows=320, chunk=640
):
    blocks, _, block_rows, _ = queries.shape
    length = sum(piece.shape[0] for piece in pieces) * block_rows
    work = blocks * block_rows * length
    scores = pltpu.VMEM((rows, length), jnp.float32)
    return pl.pallas_call(
        functools.partial(
            attention_kernel,
            piece_count=len(pieces),
            first_of=first_of,
            places=places,
            chunk=chunk,
        ),
        out_shape=jax.ShapeDtypeStruct((blocks, block_rows, HD), jnp.bfloat16),
        in_specs=[smem(), smem()] + [vmem()] * (2 + len(pieces)),
        out_specs=vmem(),
        scratch_shapes=[
            pltpu.VMEM((2 * HD, length), jnp.bfloat16),
            pltpu.VMEM((length, HD), jnp.bfloat16),
            scores,
        ],
        compiler_params=pltpu.CompilerParams(vmem_limit_bytes=VMEM_BYTES),
        cost_estimate=pl.CostEstimate(
            flops=1200 * work, bytes_accessed=3_000_000, transcendentals=work
        ),
    )(clip_lengths, levels, level_gate, queries, *pieces)


def assemble_kernel(own_ref, extra_ref, out_ref):
    for head in range(PLANE):
        out_ref[:, head * HD : (head + 1) * HD] = own_ref[head]
    for head in range(EXTRA):
        out_ref[:, (PLANE + head) * HD : (PLANE + head + 1) * HD] = extra_ref[head]


def assemble(own, extra):
    rows = own.shape[1]
    return pl.pallas_call(
        assemble_kernel,
        out_shape=jax.ShapeDtypeStruct((rows, (PLANE + EXTRA) * HD), jnp.bfloat16),
        in_specs=[vmem()] * 2,
        out_specs=vmem(),
        compiler_params=pltpu.CompilerParams(vmem_limit_bytes=SMALL_VMEM),
        cost_estimate=pl.CostEstimate(flops=0, bytes_accessed=1_700_000, transcendentals=0),
    )(own, extra)


def along_x(value, steps):
    pairs = [(source, (source + steps) % GROUP) for source in range(GROUP)]
    return lax.ppermute(value, "x", pairs)


def local(queries, keys, values, query_gain, key_gain, level_gate, clip_lengths, levels):
    own, extra = normalize(queries, keys, values, query_gain, key_gain)
    extra_held = lax.all_to_all(extra, "y", 0, 0, tiled=True)
    own_held = lax.all_to_all(own, ("x", "y"), 0, 0, tiled=True)
    pieces = [extra_held[:, 1:]]
    pieces += [along_x(pieces[0], steps) for steps in range(1, GROUP)]
    table = (clip_lengths.T, levels.T)
    row, column = lax.axis_index("x"), lax.axis_index("y")
    own_gate = lax.dynamic_slice_in_dim(level_gate, (row * EXTRA + column) * HD, HD, 1)
    extra_gate = lax.dynamic_slice_in_dim(level_gate, (PLANE + column) * HD, HD, 1)
    extra_out = attention(
        *table,
        extra_gate,
        extra_held,
        pieces,
        first_of=lambda: lax.axis_index("x") * 640,
        places=(0, 0, 1),
    )
    extra_back = lax.all_to_all(extra_out, "y", 0, 0, tiled=True)
    own_out = attention(
        *table,
        own_gate,
        own_held,
        [own_held],
        first_of=lambda: 0,
        places=(0, 1, 2),
    )
    own_back = lax.all_to_all(own_out, ("x", "y"), 0, 0, tiled=True)
    return assemble(own_back, extra_back)


def solution(mesh):
    videos = mesh.shape["seq"] // GROUP
    finer = Mesh(mesh.devices.reshape(GROUP, videos, EXTRA), ("x", "v", "y"))
    rows = P(("x", "v", "y"), None)
    return jax.shard_map(
        local,
        mesh=finer,
        in_specs=(rows, rows, rows, P(), P(), P(), P(), P()),
        out_specs=rows,
        check_vma=False,
    )
```

```python
import functools
import math

import jax
import jax.numpy as jnp
from jax import lax
from jax.experimental import pallas as pl
from jax.experimental.pallas import tpu as pltpu
from jax.sharding import Mesh
from jax.sharding import PartitionSpec as P

HD = 128
GROUP = 4
CLIPS = 4
PLANE = 32
LONGEST_CLIP = 960
STARTS = {2: (0,), 8: (0, 2, 4)}
EXTRA = 8

epsilon = 1e-06
very_negative = -1e30
exponent_scale = math.log2(math.e) / math.sqrt(HD)

VMEM_BYTES = 32 * 1024 * 1024
LARGE_VMEM = 56 * 1024 * 1024
SMALL_VMEM = 12 * 1024 * 1024


def vmem():
    return pl.BlockSpec(memory_space=pltpu.VMEM)


def smem():
    return pl.BlockSpec(memory_space=pltpu.SMEM)


def inverse_rms(ref):
    rows, width = ref.shape
    total = jnp.zeros((rows, HD), jnp.float32)
    for head in range(width // HD):
        block = ref[:, head * HD : (head + 1) * HD].astype(jnp.float32)
        total = total + block * block
    mean = jnp.sum(total, axis=1, keepdims=True) / width
    return jnp.broadcast_to(lax.rsqrt(mean + epsilon), (rows, HD))


def lay_out(q_ref, k_ref, v_ref, qg_ref, kg_ref, inverses, out_ref):
    for head in range(out_ref.shape[0]):
        columns = slice(head * HD, (head + 1) * HD)
        for part, (ref, gain_ref, inverse) in enumerate(
            ((q_ref, qg_ref, inverses[0]), (k_ref, kg_ref, inverses[1]))
        ):
            block = ref[:, columns].astype(jnp.float32)
            out_ref[head, part] = (block * inverse * gain_ref[:, columns]).astype(jnp.bfloat16)
        out_ref[head, 2] = v_ref[:, columns]


def extra_norm_kernel(q_ref, k_ref, v_ref, qg_ref, kg_ref, out_ref, inverse_ref):
    inverses = [inverse_rms(q_ref), inverse_rms(k_ref)]
    inverse_ref[0], inverse_ref[1] = inverses
    columns = slice(PLANE * HD, (PLANE + EXTRA) * HD)
    lay_out(q_ref.at[:, columns], k_ref.at[:, columns], v_ref, qg_ref, kg_ref, inverses, out_ref)


def own_norm_kernel(q_ref, k_ref, v_ref, qg_ref, kg_ref, inverse_ref, out_ref):
    inverses = [inverse_ref[0], inverse_ref[1]]
    lay_out(q_ref, k_ref, v_ref, qg_ref, kg_ref, inverses, out_ref)


def normalize(queries, keys, values, query_gain, key_gain):
    rows, width = queries.shape
    own_width, extra_width = PLANE * HD, EXTRA * HD

    def block(height, count, place=0):
        return pl.BlockSpec((height, count), lambda step: (0, place))

    def full(*shape):
        return pl.BlockSpec(shape, lambda step: (0,) * len(shape))

    whole = (queries, keys, values, query_gain[None, :], key_gain[None, :])
    params = pltpu.CompilerParams(vmem_limit_bytes=LARGE_VMEM)
    last = own_width // extra_width
    extra, inverses = pl.pallas_call(
        extra_norm_kernel,
        grid=(1,),
        out_shape=[
            jax.ShapeDtypeStruct((EXTRA, 3, rows, HD), jnp.bfloat16),
            jax.ShapeDtypeStruct((2, rows, HD), jnp.float32),
        ],
        in_specs=[block(rows, width)] * 2
        + [block(rows, extra_width, last)]
        + [block(1, extra_width, last)] * 2,
        out_specs=[full(EXTRA, 3, rows, HD), full(2, rows, HD)],
        compiler_params=params,
        cost_estimate=pl.CostEstimate(flops=3_000_000, bytes_accessed=3_000_000, transcendentals=160),
    )(*whole)
    own = pl.pallas_call(
        own_norm_kernel,
        grid=(1,),
        out_shape=jax.ShapeDtypeStruct((PLANE, 3, rows, HD), jnp.bfloat16),
        in_specs=[block(rows, own_width)] * 3 + [block(1, own_width)] * 2 + [full(2, rows, HD)],
        out_specs=full(PLANE, 3, rows, HD),
        compiler_params=params,
        cost_estimate=pl.CostEstimate(flops=3_000_000, bytes_accessed=5_000_000, transcendentals=0),
    )(*whole, inverses)
    return own, extra


def clip_of(positions, ends):
    result = jnp.zeros_like(positions)
    for boundary in range(CLIPS - 1):
        result = result + (positions >= ends[boundary]).astype(jnp.int32)
    return result


def pick(clip_ids, options):
    result = options[0]
    for clip_id in range(1, CLIPS):
        result = jnp.where(clip_ids == clip_id, options[clip_id], result)
    return result


def clip_table(lengths_ref, levels_ref):
    video = lax.axis_index("v")
    ends, total = [], 0
    for clip_id in range(CLIPS):
        total = total + lengths_ref[clip_id, video]
        ends.append(total)
    return ends, [levels_ref[clip_id, video] for clip_id in range(CLIPS)]


def blocked_rows(start, count, ends):
    clip_ids = clip_of(start + lax.broadcasted_iota(jnp.int32, (16, count), 1), ends)
    rows = lax.broadcasted_iota(jnp.int32, (16, count), 0)
    later = jnp.logical_and(clip_ids > rows, rows < CLIPS)
    return jnp.where(later, very_negative, 0.0).astype(jnp.bfloat16)


def clip_columns(clip_ids):
    lanes = lax.broadcasted_iota(jnp.int32, clip_ids.shape, 1)
    return jnp.where(clip_ids == lanes, 1.0, 0.0).astype(jnp.bfloat16)


def attention_kernel(
    lengths_ref, levels_ref, gate_ref, query_ref, *refs, piece_count, first_of, places, chunk
):
    piece_refs, (out_ref, key_ref, value_ref, *score_refs) = refs[:piece_count], refs[piece_count:]
    query_place, key_place, value_place = places
    blocks, _, block_rows, _ = query_ref.shape
    rows, _ = score_refs[0].shape
    tile_blocks, chunk_blocks = rows // block_rows, chunk // block_rows
    tiles = blocks // tile_blocks
    ends, levels = clip_table(lengths_ref, levels_ref)

    length, piece_rows = key_ref.shape[1], key_ref.shape[1] // piece_count
    for turn, piece_ref in enumerate(piece_refs):
        place = (lax.axis_index("x") + GROUP - turn) % GROUP if piece_count > 1 else 0
        for step in range(piece_rows // chunk):
            start = place * piece_rows + step * chunk
            where = pl.ds(pl.multiple_of(start, chunk), chunk)
            source = slice(step * chunk_blocks, (step + 1) * chunk_blocks)
            key_ref[0:HD, where] = piece_ref[source, key_place].reshape(chunk, HD).T
            key_ref[HD : HD + 16, where] = blocked_rows(start, chunk, ends)
            if piece_count > 1:
                value_ref[where, :] = piece_ref[source, value_place].reshape(chunk, HD)
    key_ref[HD + 16 :, :] = jnp.zeros((HD - 16, length), jnp.bfloat16)

    def values_of(step):
        if piece_count > 1:
            return value_ref[step * chunk : (step + 1) * chunk, :]
        return piece_refs[0][step * chunk_blocks : (step + 1) * chunk_blocks, value_place].reshape(chunk, HD)

    def first_row(tile):
        return first_of() + tile * rows

    def clips_of_rows(tile):
        return clip_of(first_row(tile) + lax.broadcasted_iota(jnp.int32, (rows, HD), 0), ends)

    def blocks_of(tile):
        return pl.ds(tile * tile_blocks, tile_blocks)

    def queries_of(tile):
        held = query_ref[blocks_of(tile), query_place].reshape(rows, HD)
        return jnp.concatenate([held, clip_columns(clips_of_rows(tile))], axis=1)

    def bound(tile):
        farthest = length if piece_count > 1 else (tile + 1) * rows + LONGEST_CLIP - 1
        return min(length // chunk, -(-farthest // chunk))

    gates = [jnp.where(level > 0, gate_ref[pl.ds(level, 1), :], 0.0) for level in levels]
    peaks = {}

    def score(tile, step, extended):
        here = slice(step * chunk, (step + 1) * chunk)
        scores = jnp.dot(extended, key_ref[:, here], preferred_element_type=jnp.float32)
        score_refs[tile % 2][:, here] = scores
        for part in range(chunk // HD):
            peaks[tile] = jnp.maximum(peaks[tile], scores[:, part * HD : (part + 1) * HD])

    def open_tile(tile):
        peaks[tile] = jnp.full((rows, HD), very_negative, jnp.float32)
        return queries_of(tile)

    def weigh(tile, step, peak, total, weighted):
        rounded = []
        for part in range(chunk // HD):
            start = step * chunk + part * HD
            scores = score_refs[tile % 2][:, start : start + HD]
            weights = jnp.exp2(scores * exponent_scale - peak)
            total = total + weights
            rounded.append(weights.astype(jnp.bfloat16))
        rounded = jnp.concatenate(rounded, axis=1)
        return total, weighted + jnp.dot(rounded, values_of(step), preferred_element_type=jnp.float32)

    def finish(tile, total, weighted):
        attention = weighted / jnp.sum(total, axis=1, keepdims=True)
        attention = attention.astype(jnp.bfloat16).astype(jnp.float32)
        positions = first_row(tile) + lax.broadcasted_iota(jnp.int32, (rows, HD), 0)
        gate = gates[0]
        for clip_id in range(1, CLIPS):
            gate = jnp.where(positions >= ends[clip_id - 1], gates[clip_id], gate)
        gated = (gate * attention).astype(jnp.bfloat16)
        out_ref[blocks_of(tile)] = gated.reshape(tile_blocks, block_rows, HD)

    def run(first, beyond):
        extended = open_tile(first)
        for step in range(bound(first)):
            score(first, step, extended)
        for tile in range(first, beyond):
            peak = jnp.max(peaks[tile], axis=1, keepdims=True) * exponent_scale
            peak = jnp.broadcast_to(peak, (rows, HD))
            total = jnp.zeros((rows, HD), jnp.float32)
            weighted = jnp.zeros((rows, HD), jnp.float32)
            later = bound(tile + 1) if tile + 1 < beyond else 0
            if later:
                extended = open_tile(tile + 1)
            for step in range(max(bound(tile), later)):
                if step < later:
                    score(tile + 1, step, extended)
                if step < bound(tile):
                    total, weighted = weigh(tile, step, peak, total, weighted)
            finish(tile, total, weighted)

    def clear(first, beyond):
        where = slice(first * tile_blocks, beyond * tile_blocks)
        out_ref[where] = jnp.zeros(((beyond - first) * tile_blocks, block_rows, HD), jnp.bfloat16)

    def dead(beyond):
        return pick(clip_of(first_row(beyond) - 1, ends), levels) <= 0

    for first in STARTS[tiles]:
        begins = jnp.logical_not(dead(first + 2))
        if first > 0:
            begins = dead(first) if first == STARTS[tiles][-1] else jnp.logical_and(begins, dead(first))
            pl.when(dead(first))(functools.partial(clear, first - 2, first))
        elif tiles == 2:
            pl.when(dead(2))(functools.partial(clear, 0, 2))
        pl.when(begins)(functools.partial(run, first, tiles))


def attention(
    clip_lengths, levels, level_gate, queries, pieces, first_of, places, rows=320, chunk=640
):
    blocks, _, block_rows, _ = queries.shape
    length = sum(piece.shape[0] for piece in pieces) * block_rows
    work = blocks * block_rows * length
    scores = pltpu.VMEM((rows, length), jnp.float32)
    return pl.pallas_call(
        functools.partial(
            attention_kernel,
            piece_count=len(pieces),
            first_of=first_of,
            places=places,
            chunk=chunk,
        ),
        out_shape=jax.ShapeDtypeStruct((blocks, block_rows, HD), jnp.bfloat16),
        in_specs=[smem(), smem()] + [vmem()] * (2 + len(pieces)),
        out_specs=vmem(),
        scratch_shapes=[
            pltpu.VMEM((2 * HD, length), jnp.bfloat16),
            pltpu.VMEM((length, HD), jnp.bfloat16),
            scores,
            scores,
        ],
        compiler_params=pltpu.CompilerParams(vmem_limit_bytes=VMEM_BYTES),
        cost_estimate=pl.CostEstimate(
            flops=1200 * work, bytes_accessed=3_000_000, transcendentals=work
        ),
    )(clip_lengths, levels, level_gate, queries, *pieces)


def assemble_kernel(own_ref, extra_ref, out_ref):
    for head in range(PLANE):
        out_ref[:, head * HD : (head + 1) * HD] = own_ref[head]
    for head in range(EXTRA):
        out_ref[:, (PLANE + head) * HD : (PLANE + head + 1) * HD] = extra_ref[head]


def assemble(own, extra):
    rows = own.shape[1]
    return pl.pallas_call(
        assemble_kernel,
        out_shape=jax.ShapeDtypeStruct((rows, (PLANE + EXTRA) * HD), jnp.bfloat16),
        in_specs=[vmem()] * 2,
        out_specs=vmem(),
        compiler_params=pltpu.CompilerParams(vmem_limit_bytes=SMALL_VMEM),
        cost_estimate=pl.CostEstimate(flops=0, bytes_accessed=1_700_000, transcendentals=0),
    )(own, extra)


def along_x(value, steps):
    pairs = [(source, (source + steps) % GROUP) for source in range(GROUP)]
    return lax.ppermute(value, "x", pairs)


def local(queries, keys, values, query_gain, key_gain, level_gate, clip_lengths, levels):
    own, extra = normalize(queries, keys, values, query_gain, key_gain)
    extra_held = lax.all_to_all(extra, "y", 0, 0, tiled=True)
    own_held = lax.all_to_all(own, ("x", "y"), 0, 0, tiled=True)
    pieces = [extra_held[:, 1:]]
    pieces += [along_x(pieces[0], steps) for steps in range(1, GROUP)]
    table = (clip_lengths.T, levels.T)
    row, column = lax.axis_index("x"), lax.axis_index("y")
    own_gate = lax.dynamic_slice_in_dim(level_gate, (row * EXTRA + column) * HD, HD, 1)
    extra_gate = lax.dynamic_slice_in_dim(level_gate, (PLANE + column) * HD, HD, 1)
    extra_out = attention(
        *table,
        extra_gate,
        extra_held,
        pieces,
        first_of=lambda: lax.axis_index("x") * 640,
        places=(0, 0, 1),
    )
    extra_back = lax.all_to_all(extra_out, "y", 0, 0, tiled=True)
    own_out = attention(
        *table,
        own_gate,
        own_held,
        [own_held],
        first_of=lambda: 0,
        places=(0, 1, 2),
    )
    own_back = lax.all_to_all(own_out, ("x", "y"), 0, 0, tiled=True)
    return assemble(own_back, extra_back)


def solution(mesh):
    videos = mesh.shape["seq"] // GROUP
    finer = Mesh(mesh.devices.reshape(GROUP, videos, EXTRA), ("x", "v", "y"))
    rows = P(("x", "v", "y"), None)
    return jax.shard_map(
        local,
        mesh=finer,
        in_specs=(rows, rows, rows, P(), P(), P(), P(), P()),
        out_specs=rows,
        check_vma=False,
    )
```

```python
import functools
import math

import jax
import jax.numpy as jnp
from jax import lax
from jax.experimental import pallas as pl
from jax.experimental.pallas import tpu as pltpu
from jax.sharding import Mesh
from jax.sharding import PartitionSpec as P

HD = 128
GROUP = 4
CLIPS = 4
PLANE = 32
LONGEST_CLIP = 960
STARTS = {2: (0,), 8: (0, 2, 4)}
EXTRA = 8

epsilon = 1e-06
very_negative = -1e30
exponent_scale = math.log2(math.e) / math.sqrt(HD)

VMEM_BYTES = 32 * 1024 * 1024
LARGE_VMEM = 56 * 1024 * 1024
SMALL_VMEM = 12 * 1024 * 1024


def vmem():
    return pl.BlockSpec(memory_space=pltpu.VMEM)


def smem():
    return pl.BlockSpec(memory_space=pltpu.SMEM)


def inverse_rms(ref):
    rows, width = ref.shape
    total = jnp.zeros((rows, HD), jnp.float32)
    for head in range(width // HD):
        block = ref[:, head * HD : (head + 1) * HD].astype(jnp.float32)
        total = total + block * block
    mean = jnp.sum(total, axis=1, keepdims=True) / width
    return jnp.broadcast_to(lax.rsqrt(mean + epsilon), (rows, HD))


def lay_out(q_ref, k_ref, v_ref, qg_ref, kg_ref, inverses, out_ref):
    for head in range(out_ref.shape[0]):
        columns = slice(head * HD, (head + 1) * HD)
        for part, (ref, gain_ref, inverse) in enumerate(
            ((q_ref, qg_ref, inverses[0]), (k_ref, kg_ref, inverses[1]))
        ):
            block = ref[:, columns].astype(jnp.float32)
            out_ref[head, part] = (block * inverse * gain_ref[:, columns]).astype(jnp.bfloat16)
        out_ref[head, 2] = v_ref[:, columns]


def extra_norm_kernel(q_ref, k_ref, v_ref, qg_ref, kg_ref, out_ref, inverse_ref):
    inverses = [inverse_rms(q_ref), inverse_rms(k_ref)]
    inverse_ref[0], inverse_ref[1] = inverses
    columns = slice(PLANE * HD, (PLANE + EXTRA) * HD)
    lay_out(q_ref.at[:, columns], k_ref.at[:, columns], v_ref, qg_ref, kg_ref, inverses, out_ref)


def own_norm_kernel(q_ref, k_ref, v_ref, qg_ref, kg_ref, inverse_ref, out_ref):
    inverses = [inverse_ref[0], inverse_ref[1]]
    lay_out(q_ref, k_ref, v_ref, qg_ref, kg_ref, inverses, out_ref)


def normalize(queries, keys, values, query_gain, key_gain):
    rows, width = queries.shape
    own_width, extra_width = PLANE * HD, EXTRA * HD

    def block(height, count, place=0):
        return pl.BlockSpec((height, count), lambda step: (0, place))

    def full(*shape):
        return pl.BlockSpec(shape, lambda step: (0,) * len(shape))

    whole = (queries, keys, values, query_gain[None, :], key_gain[None, :])
    params = pltpu.CompilerParams(vmem_limit_bytes=LARGE_VMEM)
    last = own_width // extra_width
    extra, inverses = pl.pallas_call(
        extra_norm_kernel,
        grid=(1,),
        out_shape=[
            jax.ShapeDtypeStruct((EXTRA, 3, rows, HD), jnp.bfloat16),
            jax.ShapeDtypeStruct((2, rows, HD), jnp.float32),
        ],
        in_specs=[block(rows, width)] * 2
        + [block(rows, extra_width, last)]
        + [block(1, extra_width, last)] * 2,
        out_specs=[full(EXTRA, 3, rows, HD), full(2, rows, HD)],
        compiler_params=params,
        cost_estimate=pl.CostEstimate(flops=3_000_000, bytes_accessed=3_000_000, transcendentals=160),
    )(*whole)
    own = pl.pallas_call(
        own_norm_kernel,
        grid=(1,),
        out_shape=jax.ShapeDtypeStruct((PLANE, 3, rows, HD), jnp.bfloat16),
        in_specs=[block(rows, own_width)] * 3 + [block(1, own_width)] * 2 + [full(2, rows, HD)],
        out_specs=full(PLANE, 3, rows, HD),
        compiler_params=params,
        cost_estimate=pl.CostEstimate(flops=3_000_000, bytes_accessed=5_000_000, transcendentals=0),
    )(*whole, inverses)
    return own, extra


def clip_of(positions, ends):
    result = jnp.zeros_like(positions)
    for boundary in range(CLIPS - 1):
        result = result + (positions >= ends[boundary]).astype(jnp.int32)
    return result


def pick(clip_ids, options):
    result = options[0]
    for clip_id in range(1, CLIPS):
        result = jnp.where(clip_ids == clip_id, options[clip_id], result)
    return result


def clip_table(lengths_ref, levels_ref):
    video = lax.axis_index("v")
    ends, total = [], 0
    for clip_id in range(CLIPS):
        total = total + lengths_ref[clip_id, video]
        ends.append(total)
    return ends, [levels_ref[clip_id, video] for clip_id in range(CLIPS)]


def blocked_rows(start, count, ends):
    clip_ids = clip_of(start + lax.broadcasted_iota(jnp.int32, (16, count), 1), ends)
    rows = lax.broadcasted_iota(jnp.int32, (16, count), 0)
    later = jnp.logical_and(clip_ids > rows, rows < CLIPS)
    return jnp.where(later, very_negative, 0.0).astype(jnp.bfloat16)


def clip_columns(clip_ids):
    lanes = lax.broadcasted_iota(jnp.int32, clip_ids.shape, 1)
    return jnp.where(clip_ids == lanes, 1.0, 0.0).astype(jnp.bfloat16)


def attention_kernel(
    lengths_ref, levels_ref, gate_ref, query_ref, *refs, piece_count, first_of, places, chunk
):
    piece_refs, (out_ref, key_ref, *score_refs) = refs[:piece_count], refs[piece_count:]
    query_place, key_place, value_place = places
    blocks, _, block_rows, _ = query_ref.shape
    rows, _ = score_refs[0].shape
    tile_blocks, chunk_blocks = rows // block_rows, chunk // block_rows
    tiles = blocks // tile_blocks
    ends, levels = clip_table(lengths_ref, levels_ref)

    length = key_ref.shape[1]
    piece_chunks = length // chunk // piece_count

    def fill(step):
        turn, part = step // piece_chunks, step % piece_chunks
        source = slice(part * chunk_blocks, (part + 1) * chunk_blocks)
        where = slice(step * chunk, (step + 1) * chunk)
        place = (lax.axis_index("x") + GROUP - turn) % GROUP if piece_count > 1 else turn
        start = (place * piece_chunks + part) * chunk
        key_ref[0:HD, where] = piece_refs[turn][source, key_place].reshape(chunk, HD).T
        key_ref[HD : HD + 16, where] = blocked_rows(start, chunk, ends)
        key_ref[HD + 16 :, where] = jnp.zeros((HD - 16, chunk), jnp.bfloat16)

    def values_of(step):
        turn, part = step // piece_chunks, step % piece_chunks
        source = slice(part * chunk_blocks, (part + 1) * chunk_blocks)
        return piece_refs[turn][source, value_place].reshape(chunk, HD)

    def first_row(tile):
        return first_of() + tile * rows

    def clips_of_rows(tile):
        return clip_of(first_row(tile) + lax.broadcasted_iota(jnp.int32, (rows, HD), 0), ends)

    def blocks_of(tile):
        return pl.ds(tile * tile_blocks, tile_blocks)

    def queries_of(tile):
        held = query_ref[blocks_of(tile), query_place].reshape(rows, HD)
        return jnp.concatenate([held, clip_columns(clips_of_rows(tile))], axis=1)

    def bound(tile):
        farthest = length if piece_count > 1 else (tile + 1) * rows + LONGEST_CLIP - 1
        return min(length // chunk, -(-farthest // chunk))

    gates = [jnp.where(level > 0, gate_ref[pl.ds(level, 1), :], 0.0) for level in levels]
    peaks = {}

    def score(tile, step, extended, filled):
        if step not in filled:
            fill(step)
            filled.append(step)
        here = slice(step * chunk, (step + 1) * chunk)
        scores = jnp.dot(extended, key_ref[:, here], preferred_element_type=jnp.float32)
        score_refs[tile % 2][:, here] = scores
        for part in range(chunk // HD):
            peaks[tile] = jnp.maximum(peaks[tile], scores[:, part * HD : (part + 1) * HD])

    def open_tile(tile):
        peaks[tile] = jnp.full((rows, HD), very_negative, jnp.float32)
        return queries_of(tile)

    def weigh(tile, step, peak, total, weighted):
        rounded = []
        for part in range(chunk // HD):
            start = step * chunk + part * HD
            scores = score_refs[tile % 2][:, start : start + HD]
            weights = jnp.exp2(scores * exponent_scale - peak)
            total = total + weights
            rounded.append(weights.astype(jnp.bfloat16))
        rounded = jnp.concatenate(rounded, axis=1)
        return total, weighted + jnp.dot(rounded, values_of(step), preferred_element_type=jnp.float32)

    def finish(tile, total, weighted):
        attention = weighted / jnp.sum(total, axis=1, keepdims=True)
        attention = attention.astype(jnp.bfloat16).astype(jnp.float32)
        positions = first_row(tile) + lax.broadcasted_iota(jnp.int32, (rows, HD), 0)
        gate = gates[0]
        for clip_id in range(1, CLIPS):
            gate = jnp.where(positions >= ends[clip_id - 1], gates[clip_id], gate)
        gated = (gate * attention).astype(jnp.bfloat16)
        out_ref[blocks_of(tile)] = gated.reshape(tile_blocks, block_rows, HD)

    def run(first, beyond):
        filled = []
        extended = open_tile(first)
        for step in range(bound(first)):
            score(first, step, extended, filled)
        for tile in range(first, beyond):
            peak = jnp.max(peaks[tile], axis=1, keepdims=True) * exponent_scale
            peak = jnp.broadcast_to(peak, (rows, HD))
            total = jnp.zeros((rows, HD), jnp.float32)
            weighted = jnp.zeros((rows, HD), jnp.float32)
            later = bound(tile + 1) if tile + 1 < beyond else 0
            if later:
                extended = open_tile(tile + 1)
            for step in range(max(bound(tile), later)):
                if step < later:
                    score(tile + 1, step, extended, filled)
                if step < bound(tile):
                    total, weighted = weigh(tile, step, peak, total, weighted)
            finish(tile, total, weighted)

    def clear(first, beyond):
        where = slice(first * tile_blocks, beyond * tile_blocks)
        out_ref[where] = jnp.zeros(((beyond - first) * tile_blocks, block_rows, HD), jnp.bfloat16)

    def dead(beyond):
        return pick(clip_of(first_row(beyond) - 1, ends), levels) <= 0

    for first in STARTS[tiles]:
        begins = jnp.logical_not(dead(first + 2))
        if first > 0:
            begins = dead(first) if first == STARTS[tiles][-1] else jnp.logical_and(begins, dead(first))
            pl.when(dead(first))(functools.partial(clear, first - 2, first))
        elif tiles == 2:
            pl.when(dead(2))(functools.partial(clear, 0, 2))
        pl.when(begins)(functools.partial(run, first, tiles))


def attention(
    clip_lengths, levels, level_gate, queries, pieces, first_of, places, rows=320, chunk=640
):
    blocks, _, block_rows, _ = queries.shape
    length = sum(piece.shape[0] for piece in pieces) * block_rows
    work = blocks * block_rows * length
    scores = pltpu.VMEM((rows, length), jnp.float32)
    return pl.pallas_call(
        functools.partial(
            attention_kernel,
            piece_count=len(pieces),
            first_of=first_of,
            places=places,
            chunk=chunk,
        ),
        out_shape=jax.ShapeDtypeStruct((blocks, block_rows, HD), jnp.bfloat16),
        in_specs=[smem(), smem()] + [vmem()] * (2 + len(pieces)),
        out_specs=vmem(),
        scratch_shapes=[
            pltpu.VMEM((2 * HD, length), jnp.bfloat16),
            scores,
            scores,
        ],
        compiler_params=pltpu.CompilerParams(vmem_limit_bytes=VMEM_BYTES),
        cost_estimate=pl.CostEstimate(
            flops=1200 * work, bytes_accessed=3_000_000, transcendentals=work
        ),
    )(clip_lengths, levels, level_gate, queries, *pieces)


def assemble_kernel(own_ref, extra_ref, out_ref):
    for head in range(PLANE):
        out_ref[:, head * HD : (head + 1) * HD] = own_ref[head]
    for head in range(EXTRA):
        out_ref[:, (PLANE + head) * HD : (PLANE + head + 1) * HD] = extra_ref[head]


def assemble(own, extra):
    rows = own.shape[1]
    return pl.pallas_call(
        assemble_kernel,
        out_shape=jax.ShapeDtypeStruct((rows, (PLANE + EXTRA) * HD), jnp.bfloat16),
        in_specs=[vmem()] * 2,
        out_specs=vmem(),
        compiler_params=pltpu.CompilerParams(vmem_limit_bytes=SMALL_VMEM),
        cost_estimate=pl.CostEstimate(flops=0, bytes_accessed=1_700_000, transcendentals=0),
    )(own, extra)


def along_x(value, steps):
    pairs = [(source, (source + steps) % GROUP) for source in range(GROUP)]
    return lax.ppermute(value, "x", pairs)


def local(queries, keys, values, query_gain, key_gain, level_gate, clip_lengths, levels):
    own, extra = normalize(queries, keys, values, query_gain, key_gain)
    extra_held = lax.all_to_all(extra, "y", 0, 0, tiled=True)
    own_held = lax.all_to_all(own, ("x", "y"), 0, 0, tiled=True)
    pieces = [extra_held[:, 1:]]
    pieces += [along_x(pieces[0], steps) for steps in range(1, GROUP)]
    table = (clip_lengths.T, levels.T)
    row, column = lax.axis_index("x"), lax.axis_index("y")
    own_gate = lax.dynamic_slice_in_dim(level_gate, (row * EXTRA + column) * HD, HD, 1)
    extra_gate = lax.dynamic_slice_in_dim(level_gate, (PLANE + column) * HD, HD, 1)
    extra_out = attention(
        *table,
        extra_gate,
        extra_held,
        pieces,
        first_of=lambda: lax.axis_index("x") * 640,
        places=(0, 0, 1),
    )
    extra_back = lax.all_to_all(extra_out, "y", 0, 0, tiled=True)
    own_out = attention(
        *table,
        own_gate,
        own_held,
        [own_held],
        first_of=lambda: 0,
        places=(0, 1, 2),
    )
    own_back = lax.all_to_all(own_out, ("x", "y"), 0, 0, tiled=True)
    return assemble(own_back, extra_back)


def solution(mesh):
    videos = mesh.shape["seq"] // GROUP
    finer = Mesh(mesh.devices.reshape(GROUP, videos, EXTRA), ("x", "v", "y"))
    rows = P(("x", "v", "y"), None)
    return jax.shard_map(
        local,
        mesh=finer,
        in_specs=(rows, rows, rows, P(), P(), P(), P(), P()),
        out_specs=rows,
        check_vma=False,
    )
```
